256 devices in a mesh: dp: 16 (over z, core), ctx: 16 (over y, x).
Axes of the slice: x: 4, y: 4, z: 8, core: 2. Of those that a mesh axis runs over, the one named last changes fastest.
Arguments:
- queries_in: bfloat16 [16, 16, 128, 2048], P('dp', None, 'ctx'), may hold values from -100 to 100
- keys_in: bfloat16 [16, 16, 128, 2048], P('dp', None, 'ctx'), may hold values from -4 to 4
- values_in: bfloat16 [16, 16, 128, 2048], P('dp', None, 'ctx'), may hold values from -6 to 6
- upstream: bfloat16 [16, 2048, 2048], P('dp', 'ctx'), may hold values from -6 to 6
- lengths: int32 [16], replicated, may hold values from 256 to 2048, as said below
- assignment: int32 [16], replicated, may hold values from 0 to 15, each once
- span_order: int32 [16, 256], replicated, may hold values from 0 to 255, as said below
Outputs:
- attended: bfloat16 [16, 2048, 2048], P('dp', 'ctx')
- query_grad: bfloat16 [16, 2048, 2048], P('dp', 'ctx')
- key_grad: bfloat16 [16, 2048, 2048], P('dp', 'ctx')
- value_grad: bfloat16 [16, 2048, 2048], P('dp', 'ctx')
The draws below stay inside these ranges and needn't reach their ends.
Inputs may be any that keep to these rules, and one draw needn't show every extreme that they name: `lengths`: one episode has exactly 2048 tokens. `span_order`: for each episode one of two layouts is drawn: span s * 16 + c sits at block c * 16 + s, or at block c * 8 + s for s < 8 and at (31 - c) * 8 + s - 8 otherwise.
All inputs are finite; a program needn't handle non-finite values.
Results may differ from the reference program's by a relative error of at most 0.03.
Values may be sent and summed in bfloat16 or wider, within the bound.
A program may use at most 192 MiB of HBM per device.

```python
import math
import jax
import jax.numpy as jnp
from jax import lax

HEADS = 16
HEAD_DIM = 128
EPISODES = 16
LEN = 2048
PIECE = 128
SPAN = 8
FEAT = 2048
N_DP = 16
N_CTX = 16


def key_base(key):
    drawn = jax.random.normal(jax.random.fold_in(key, 11), (N_DP, EPISODES, N_CTX, SPAN, FEAT), jnp.float32)
    return jnp.clip(1.5 * drawn, -4.0, 4.0)


def draw_keys_in(key, part):
    base = key_base(key)
    return base.reshape(N_DP, EPISODES, PIECE, FEAT).astype(jnp.bfloat16)


def draw_queries_in(key, part):
    key = jax.random.fold_in(key, 3)
    drawn = jax.random.normal(key, (N_DP, EPISODES, N_CTX, SPAN, FEAT), jnp.float32)
    result = jnp.clip(1.5 * drawn, -4.0, 4.0)
    return result.reshape(N_DP, EPISODES, PIECE, FEAT).astype(jnp.bfloat16)


def draw_lengths(key, part):
    key = jax.random.fold_in(key, 7)
    first, second = jax.random.split(key)
    drawn = jax.random.randint(first, (EPISODES,), LEN // 8, LEN + 1)
    longest = jax.random.randint(second, (), 0, EPISODES)
    return jnp.where(jnp.arange(EPISODES) == longest, LEN, drawn).astype(jnp.int32)


def draw_span_order(key, part):
    key = jax.random.fold_in(key, 9)
    layouts = jax.random.randint(key, (EPISODES, 1, 1), 0, 2)
    stripe = jnp.arange(N_DP)[None, :, None]
    column = jnp.arange(N_CTX)[None, None, :]
    halfway = N_DP // 2
    direct = column * N_DP + stripe
    folded = jnp.where(stripe < halfway, column * halfway + stripe, (2 * N_CTX - 1 - column) * halfway + stripe - halfway)
    chosen = jnp.where(layouts == 0, direct, folded)
    return chosen.reshape(EPISODES, N_DP * N_CTX).astype(jnp.int32)


def level_of(rng, extent, cuts, least, top_value):
    def one(axis_at, shards_of):
        heights = jax.random.uniform(jax.random.fold_in(jax.random.fold_in(rng, 6), axis_at), (shards_of,), jnp.float32, least / len(cuts), top_value / len(cuts))
        return jnp.repeat(jnp.exp(heights), extent[axis_at] // shards_of).reshape((-1,) + (1,) * (len(extent) - axis_at - 1))

    gain = one(*cuts[0])
    for cut in cuts[1:]:
        gain = gain * one(*cut)
    return gain


def gaussian(stream_key, shape, scale, reach, cuts=(), kind=jnp.bfloat16):
    level = level_of(stream_key, shape, cuts, -0.22, 0.18) if cuts else 1.0
    values = jax.random.normal(stream_key, shape, jnp.float32) * scale * level
    return jnp.minimum(jnp.maximum(values, -reach), reach).astype(kind)


def setup_inputs(seed: int = 0) -> dict:
    keys = jax.random.split(jax.random.key(seed), 8)
    queries_in = draw_queries_in(jax.random.fold_in(keys[7], 71), 0)
    keys_in = draw_keys_in(jax.random.fold_in(keys[7], 71), 0)
    values_in = gaussian(keys[2], (N_DP, EPISODES, PIECE, FEAT), 1.0, 6.0, ((0, 16), (2, 16)))
    upstream = gaussian(keys[3], (EPISODES, LEN, FEAT), 1.0, 6.0, ((0, 16), (1, 16)))
    lengths = draw_lengths(jax.random.fold_in(keys[7], 71), 0)
    assignment = jax.random.permutation(keys[5], EPISODES).astype(jnp.int32)
    span_order = draw_span_order(jax.random.fold_in(keys[7], 71), 0)
    return {"queries_in": queries_in, "keys_in": keys_in, "values_in": values_in, "upstream": upstream, "lengths": lengths, "assignment": assignment, "span_order": span_order}


masked_value = -1e+30

def arrange(array, episode):
    picked = lax.dynamic_index_in_dim(array, episode, 1, keepdims=False)
    picked = picked.reshape(N_DP, N_CTX, SPAN, FEAT).transpose(1, 0, 2, 3)
    return picked.reshape(LEN, HEADS, HEAD_DIM)

def reference(queries_in, keys_in, values_in, upstream, lengths, assignment, span_order):
    labels = jnp.arange(EPISODES, dtype=jnp.int32)
    sources = lax.optimization_barrier(jnp.sum(jnp.where(assignment[None, :] == labels[:, None], labels[None, :], 0), axis=1)).astype(jnp.int32)
    offsets = jnp.arange(SPAN, dtype=jnp.int32)
    scaling = 1.0 / math.sqrt(HEAD_DIM)

    def per_shard(shard):
        episode = sources[shard]
        query_wide = arrange(queries_in, episode).astype(jnp.float32)
        key_wide = arrange(keys_in, episode).astype(jnp.float32)
        value_wide = arrange(values_in, episode).astype(jnp.float32)
        given = lax.dynamic_index_in_dim(upstream, shard, 0, keepdims=False).reshape(LEN, HEADS, HEAD_DIM)
        length = lengths[episode]
        layout = lax.dynamic_index_in_dim(span_order, episode, 0, keepdims=False).reshape(N_DP, N_CTX)
        places = (layout.T[:, :, None] * SPAN + offsets).reshape(LEN)
        alive = places < length
        visible = (places[None, :] <= places[:, None]) & alive[None, :]
        scores = jnp.einsum('qhd,khd->hqk', query_wide, key_wide) * scaling
        scores = jnp.where(visible[None], scores, masked_value)
        peak = lax.optimization_barrier(jnp.max(scores, axis=2))
        weights = jnp.exp(scores - peak[:, :, None])
        totals = lax.optimization_barrier(jnp.sum(weights, axis=2))
        rounded = lax.optimization_barrier(weights.astype(jnp.bfloat16)).astype(jnp.float32)
        blended = jnp.einsum('hqk,khd->qhd', rounded, value_wide) / totals.T[:, :, None]
        attended = jnp.where(alive[:, None, None], blended, 0.0).astype(jnp.bfloat16)
        log_total = peak + jnp.log(totals)
        incoming = jnp.where(alive[:, None, None], given, jnp.zeros_like(given))
        incoming_wide = incoming.astype(jnp.float32)
        row_dots = lax.optimization_barrier(jnp.sum(incoming_wide * attended.astype(jnp.float32), axis=2))
        probs = jnp.exp(scores - log_total[:, :, None])
        dweights = jnp.einsum('qhd,khd->hqk', incoming_wide, value_wide)
        dscores = probs * (dweights - row_dots.T[:, :, None])
        dscore_round = lax.optimization_barrier(dscores.astype(jnp.bfloat16)).astype(jnp.float32)
        prob_round = lax.optimization_barrier(probs.astype(jnp.bfloat16)).astype(jnp.float32)
        query_grad = jnp.einsum('hqk,khd->qhd', dscore_round, key_wide) * scaling
        key_grad = jnp.einsum('hqk,qhd->khd', dscore_round, query_wide) * scaling
        value_grad = jnp.einsum('hqk,qhd->khd', prob_round, incoming_wide)
        return (attended.reshape(LEN, FEAT), query_grad.astype(jnp.bfloat16).reshape(LEN, FEAT), key_grad.astype(jnp.bfloat16).reshape(LEN, FEAT), value_grad.astype(jnp.bfloat16).reshape(LEN, FEAT))
    results = lax.map(per_shard, labels)
    return (results[0], results[1], results[2], results[3])
```

```python
import math

import jax
import jax.numpy as jnp
from jax import lax
from jax.experimental import pallas as pl
from jax.experimental.pallas import tpu as pltpu
from jax.sharding import PartitionSpec as P

MESH = pl.DeviceIdType.MESH
N = 16
DIM = 128
ROWS = 128
LEN = 2048
FEAT = 2048
SPAN = 8
CHUNK = 64
BLOCK = 512
SCALE = 1.0 / math.sqrt(DIM)
LOG2E = math.log2(math.e)
MASKED = -1e30
ROWS_BY_ROWS = (((1,), (1,)), ((), ()))
ROWS_BY_COLUMNS = (((1,), (0,)), ((), ()))


def dot(left, right, dims):
    return lax.dot_general(left, right, dims, preferred_element_type=jnp.float32)


def partner(me, i):
    step = jnp.where(i % 2 == 1, (i + 1) // 2, N - i // 2)
    return lax.rem(me + step, N)


def kernel(
    assignment, lengths, span_order, keys_in, queries_in, values_in, upstream,
    attended, query_grad, key_grad, value_grad,
    sources, held_k, held_q, held_v, staged, landed, regrouped, arrived_k, arrived_q, arrived_v, arrived_g,
    ordered, weights, inverse,
    key_sum, value_sum, results, leaving,
    held_sem, up_sem, send_one, recv_one, send_two, recv_two, send_out, recv_out, own_sem,
):
    shard = lax.axis_index("dp")
    column = lax.axis_index("ctx")
    ins = (keys_in, queries_in, values_in)
    outs = (attended, query_grad, key_grad, value_grad)
    held = (held_k, held_q, held_v)
    arrived = (arrived_k, arrived_q, arrived_v, arrived_g)

    loads = [pltpu.make_async_copy(ins[a], held[a], held_sem.at[a]) for a in range(3)]
    for load in loads:
        load.start()

    barrier = pltpu.get_barrier_semaphore()

    def greet(k, carry):
        pl.semaphore_signal(barrier, inc=1, device_id=(lax.rem(shard + k, N), column), device_id_type=MESH)
        pl.semaphore_signal(barrier, inc=1, device_id=(shard, lax.rem(column + k, N)), device_id_type=MESH)
        return carry

    lax.fori_loop(1, N, greet, 0)

    def find(d, carry):
        found = jnp.int32(0)
        for e in range(N):
            found = found + e * (assignment[e] == d).astype(jnp.int32)
        sources[d] = jnp.minimum(found, N - 1)
        return carry

    lax.fori_loop(0, N, find, 0)
    episode = sources[shard]
    length = lengths[episode]
    folded = jnp.clip(2 - lax.div(span_order[episode, 1], SPAN), 0, 1)
    pl.semaphore_wait(barrier, 2 * (N - 1))

    def send_upstream(i, carry):
        to = partner(column, i)
        pltpu.make_async_remote_copy(
            src_ref=upstream.at[:, :, pl.ds(pl.multiple_of(to * DIM, DIM), DIM)],
            dst_ref=arrived[3].at[column],
            send_sem=send_two.at[3],
            recv_sem=recv_two.at[3],
            device_id=(shard, to),
            device_id_type=MESH,
        ).start()
        return carry

    lax.fori_loop(1, N, send_upstream, 0)
    own_up = pltpu.make_async_copy(
        upstream.at[:, :, pl.ds(pl.multiple_of(column * DIM, DIM), DIM)], arrived[3].at[column], up_sem
    )
    own_up.start()

    def by_head(a, to):
        e = sources[to]
        pair = held[a][lax.div(e, 2)].astype(jnp.float32)
        odd = jnp.full((SPAN, FEAT), lax.rem(e, 2), jnp.int32) == 1
        rows = jnp.where(odd, pair[SPAN:], pair[:SPAN])
        heads = [rows[:, h * DIM : (h + 1) * DIM] for h in range(N)]
        return jnp.concatenate(heads, axis=0).astype(jnp.bfloat16)

    def first(a):
        loads[a].wait()

        def send(i, carry):
            to = partner(shard, i)
            staged[a, to] = by_head(a, to)
            pltpu.make_async_remote_copy(
                src_ref=staged.at[a, to],
                dst_ref=landed.at[a, shard],
                send_sem=send_one.at[a],
                recv_sem=recv_one.at[a],
                device_id=(to, column),
                device_id_type=MESH,
            ).start()
            return carry

        lax.fori_loop(1, N, send, 0)
        landed[a, shard] = by_head(a, shard)

    def wait_all(buffer, send_sem, recv_sem):
        whole = pltpu.make_async_remote_copy(
            src_ref=buffer,
            dst_ref=buffer,
            send_sem=send_sem,
            recv_sem=recv_sem,
            device_id=(shard, column),
            device_id_type=MESH,
        )
        whole.wait_recv()
        whole.wait_send()

    def second(a):
        wait_all(landed.at[a, pl.ds(0, N - 1)], send_one.at[a], recv_one.at[a])

        def regroup(pair, carry):
            both = landed[a, :, pl.ds(pl.multiple_of(pair * 16, 16), 16), :].astype(jnp.float32)
            regrouped[a, 2 * pair] = both[:, :SPAN].reshape(2, CHUNK, DIM).astype(jnp.bfloat16)
            regrouped[a, 2 * pair + 1] = both[:, SPAN:].reshape(2, CHUNK, DIM).astype(jnp.bfloat16)
            return carry

        lax.fori_loop(0, N // 2, regroup, 0)

        def send(i, carry):
            to = partner(column, i)
            pltpu.make_async_remote_copy(
                src_ref=regrouped.at[a, to],
                dst_ref=arrived[a].at[column],
                send_sem=send_two.at[a],
                recv_sem=recv_two.at[a],
                device_id=(shard, to),
                device_id_type=MESH,
            ).start()
            return carry

        lax.fori_loop(1, N, send, 0)
        arrived[a][column] = regrouped[a, column]

    def order(a):
        wait_all(arrived[a].at[pl.ds(0, N - 1)], send_two.at[a], recv_two.at[a])

        def place(p, carry):
            second_half = p // N
            piece = p // 2 + folded * (p + second_half * (2 * N - 1 - 2 * p) - p // 2)
            half = p % 2 + folded * (second_half - p % 2)
            ordered[a, pl.ds(pl.multiple_of(p * CHUNK, CHUNK), CHUNK), :] = arrived[a][piece, half]
            return carry

        lax.fori_loop(0, 2 * N, place, 0)

    def give(a):
        def send(i, carry):
            to = partner(column, i)
            low = 2 * to - folded * to
            high = 2 * to + 1 + folded * (2 * N - 2 - 3 * to)
            leaving[a, to, :CHUNK] = results[a, low]
            leaving[a, to, CHUNK:] = results[a, high]
            return carry

        lax.fori_loop(0, N, send, 0)
        own_columns = pl.ds(pl.multiple_of(column * DIM, DIM), DIM)

        def start(i, carry):
            to = partner(column, i)
            pltpu.make_async_remote_copy(
                src_ref=leaving.at[a, to],
                dst_ref=outs[a].at[:, own_columns],
                send_sem=send_out.at[a],
                recv_sem=recv_out.at[a],
                device_id=(shard, to),
                device_id_type=MESH,
            ).start()
            return carry

        lax.fori_loop(1, N, start, 0)
        own = pltpu.make_async_copy(leaving.at[a, column], outs[a].at[:, own_columns], own_sem.at[a])
        own.start()
        return own

    first(0)
    first(1)
    first(2)
    second(0)
    second(1)
    own_up.wait()
    order(3)
    order(0)
    order(1)

    keys, queries, values, given = (ordered.at[a] for a in range(4))
    blocks = LEN // BLOCK
    for b in range(blocks):
        start, stop = b * BLOCK, (b + 1) * BLOCK
        scores = dot(queries[start:stop], keys[:stop], ROWS_BY_ROWS)
        row = lax.broadcasted_iota(jnp.int32, (BLOCK, BLOCK), 0)
        col = lax.broadcasted_iota(jnp.int32, (BLOCK, BLOCK), 1)
        last = jnp.where(col <= row, scores[:, start:], MASKED)
        scores = jnp.concatenate([scores[:, :start], last], axis=1) if b else last
        peak = jnp.max(scores, axis=1, keepdims=True)
        block_weights = jnp.exp2((scores - peak) * (SCALE * LOG2E))
        inverse[start:stop] = 1.0 / jnp.sum(block_weights, axis=1, keepdims=True)
        weights[start:stop, :stop] = block_weights.astype(jnp.bfloat16)

    second(2)
    order(2)

    def chunks(b):
        return slice(b * (BLOCK // CHUNK), (b + 1) * (BLOCK // CHUNK))

    def keep(a, b, rows):
        results[a, chunks(b)] = rows.astype(jnp.bfloat16).reshape(BLOCK // CHUNK, CHUNK, DIM)

    def alive(start):
        return start + lax.broadcasted_iota(jnp.int32, (BLOCK, 1), 0) < length

    for b in range(blocks):
        start, stop = b * BLOCK, (b + 1) * BLOCK
        blended = dot(weights[start:stop, :stop], values[:stop], ROWS_BY_COLUMNS) * inverse[start:stop]
        keep(0, b, jnp.where(alive(start), blended, 0.0))
    own = [give(0)]

    for b in reversed(range(blocks)):
        start, stop = b * BLOCK, (b + 1) * BLOCK
        block_weights = weights[start:stop, :stop]
        scale = inverse[start:stop]
        incoming = jnp.where(alive(start), given[start:stop].astype(jnp.float32), 0.0)
        row_dots = jnp.sum(incoming * results[0, chunks(b)].reshape(BLOCK, DIM).astype(jnp.float32), axis=1, keepdims=True)
        dweights = dot(incoming.astype(jnp.bfloat16), values[:stop], ROWS_BY_ROWS)
        dscores = (block_weights.astype(jnp.float32) * (dweights - row_dots)).astype(jnp.bfloat16)
        query_term = dot(dscores, keys[:stop], ROWS_BY_COLUMNS) * (scale * SCALE)
        keep(1, b, query_term)
        scaled_queries = (queries[start:stop].astype(jnp.float32) * scale).T.astype(jnp.bfloat16)
        scaled_incoming = (incoming * scale).T.astype(jnp.bfloat16)
        key_term = dot(scaled_queries, dscores, ROWS_BY_COLUMNS)
        value_term = dot(scaled_incoming, block_weights, ROWS_BY_COLUMNS)
        if b == blocks - 1:
            key_sum[:, :stop] = key_term
            value_sum[:, :stop] = value_term
        else:
            key_sum[:, :stop] += key_term
            value_sum[:, :stop] += value_term
        keep(2, b, (key_sum[:, start:stop] * SCALE).T)
        keep(3, b, value_sum[:, start:stop].T)

    own += [give(1), give(2), give(3)]
    for a in range(4):
        own[a].wait()
        wait_all(outs[a].at[:, pl.ds(0, (N - 1) * DIM)], send_out.at[a], recv_out.at[a])


def per_device(queries_in, keys_in, values_in, upstream, lengths, assignment, span_order):
    flat = [x.reshape(N // 2, 2 * SPAN, FEAT) for x in (keys_in, queries_in, values_in)]
    smem = pl.BlockSpec(memory_space=pltpu.SMEM)
    anywhere = pl.BlockSpec(memory_space=pl.ANY)
    bf16, f32 = jnp.bfloat16, jnp.float32
    results = pl.pallas_call(
        kernel,
        out_shape=[jax.ShapeDtypeStruct((ROWS, FEAT), bf16)] * 4,
        in_specs=[smem] * 3 + [anywhere] * 4,
        out_specs=[anywhere] * 4,
        scratch_shapes=[
            pltpu.SMEM((N,), jnp.int32),
            pltpu.VMEM((N // 2, 2 * SPAN, FEAT), bf16),
            pltpu.VMEM((N // 2, 2 * SPAN, FEAT), bf16),
            pltpu.VMEM((N // 2, 2 * SPAN, FEAT), bf16),
            pltpu.VMEM((3, N, ROWS, DIM), bf16),
            pltpu.VMEM((3, N, ROWS, DIM), bf16),
            pltpu.VMEM((3, N, 2, CHUNK, DIM), bf16),
            pltpu.VMEM((N, 2, CHUNK, DIM), bf16),
            pltpu.VMEM((N, 2, CHUNK, DIM), bf16),
            pltpu.VMEM((N, 2, CHUNK, DIM), bf16),
            pltpu.VMEM((N, 2, CHUNK, DIM), bf16),
            pltpu.VMEM((4, LEN, DIM), bf16),
            pltpu.VMEM((LEN, LEN), bf16),
            pltpu.VMEM((LEN, 1), f32),
            pltpu.VMEM((DIM, LEN), f32),
            pltpu.VMEM((DIM, LEN), f32),
            pltpu.VMEM((4, LEN // CHUNK, CHUNK, DIM), bf16),
            pltpu.VMEM((4, N, ROWS, DIM), bf16),
            pltpu.SemaphoreType.DMA((3,)),
            pltpu.SemaphoreType.DMA,
            pltpu.SemaphoreType.DMA((3,)),
            pltpu.SemaphoreType.DMA((3,)),
            pltpu.SemaphoreType.DMA((4,)),
            pltpu.SemaphoreType.DMA((4,)),
            pltpu.SemaphoreType.DMA((4,)),
            pltpu.SemaphoreType.DMA((4,)),
            pltpu.SemaphoreType.DMA((4,)),
        ],
        compiler_params=pltpu.CompilerParams(
            collective_id=0, has_side_effects=True, vmem_limit_bytes=56 * 1024 * 1024
        ),
    )(assignment, lengths, span_order, *flat, upstream.reshape(2, CHUNK, FEAT))
    return tuple(x.reshape(1, ROWS, FEAT) for x in results)


def solution(mesh):
    split = P("dp", None, "ctx", None)
    rows = P("dp", "ctx", None)
    return jax.shard_map(
        per_device,
        mesh=mesh,
        in_specs=(split, split, split, rows, P(), P(), P()),
        out_specs=(rows,) * 4,
        check_vma=False,
    )
```

```python
import functools
import math

import jax
import jax.numpy as jnp
from jax import lax
from jax.experimental import pallas as pl
from jax.experimental.pallas import tpu as pltpu
from jax.sharding import PartitionSpec as P

MESH = pl.DeviceIdType.MESH
N = 16
DIM = 128
ROWS = 128
LEN = 2048
FEAT = 2048
SPAN = 8
CHUNK = 64
BLOCK = 512
WINDOW = 2
FORWARD = 3
ORDER = ((0, 0), (1, 0), (2, 0), (0, 1), (1, 1), (2, 1))
SCALE = 1.0 / math.sqrt(DIM)
LOG2E = math.log2(math.e)
MASKED = -1e30
ROWS_BY_ROWS = (((1,), (1,)), ((), ()))
ROWS_BY_COLUMNS = (((1,), (0,)), ((), ()))


def dot(left, right, dims):
    return lax.dot_general(left, right, dims, preferred_element_type=jnp.float32)


def partner(me, i):
    step = jnp.where(i % 2 == 1, (i + 1) // 2, N - i // 2)
    return lax.rem(me + step, N)


def kernel(
    assignment, lengths, span_order, keys_in, queries_in, values_in, upstream,
    attended, query_grad, key_grad, value_grad,
    sources, held_k, held_q, held_v, staged, landed, regrouped, arrived_k, arrived_q, arrived_v, arrived_g,
    ordered, weights, inverse,
    key_sum, value_sum, results, leaving,
    held_sem, up_sem, send_one, send_sibling, recv_one, send_two, recv_two, send_out, recv_out, own_sem,
):
    shard = lax.axis_index("dp")
    column = lax.axis_index("ctx")
    ins = (keys_in, queries_in, values_in)
    outs = (attended, query_grad, key_grad, value_grad)
    held = (held_k, held_q, held_v)
    arrived = (arrived_k, arrived_q, arrived_v, arrived_g)

    loads = [pltpu.make_async_copy(ins[a], held[a], held_sem.at[a]) for a in range(3)]
    for load in loads:
        load.start()

    barrier = pltpu.get_barrier_semaphore()

    def greet(k, carry):
        pl.semaphore_signal(barrier, inc=1, device_id=(lax.rem(shard + k, N), column), device_id_type=MESH)
        pl.semaphore_signal(barrier, inc=1, device_id=(shard, lax.rem(column + k, N)), device_id_type=MESH)
        return carry

    lax.fori_loop(1, N, greet, 0)

    def find(d, carry):
        found = jnp.int32(0)
        for e in range(N):
            found = found + e * (assignment[e] == d).astype(jnp.int32)
        sources[d] = jnp.minimum(found, N - 1)
        return carry

    lax.fori_loop(0, N, find, 0)
    episode = sources[shard]
    length = lengths[episode]
    folded = jnp.clip(2 - lax.div(span_order[episode, 1], SPAN), 0, 1)
    pl.semaphore_wait(barrier, 2 * (N - 1))

    def send_upstream(i, carry):
        to = partner(column, i)
        pltpu.make_async_remote_copy(
            src_ref=upstream.at[:, :, pl.ds(pl.multiple_of(to * DIM, DIM), DIM)],
            dst_ref=arrived[3].at[column],
            send_sem=send_two.at[3],
            recv_sem=recv_two.at[3],
            device_id=(shard, to),
            device_id_type=MESH,
        ).start()
        return carry

    lax.fori_loop(1, N, send_upstream, 0)
    own_up = pltpu.make_async_copy(
        upstream.at[:, :, pl.ds(pl.multiple_of(column * DIM, DIM), DIM)], arrived[3].at[column], up_sem
    )
    own_up.start()

    def by_head(a, to):
        e = sources[to]
        pair = held[a][lax.div(e, 2)].astype(jnp.float32)
        odd = jnp.full((SPAN, FEAT), lax.rem(e, 2), jnp.int32) == 1
        rows = jnp.where(odd, pair[SPAN:], pair[:SPAN])
        heads = [rows[:, h * DIM : (h + 1) * DIM] for h in range(N)]
        return jnp.concatenate(heads, axis=0).astype(jnp.bfloat16)

    core = lax.rem(shard, 2)
    chip = lax.div(shard, 2)

    def first(a, side):
        def send(to, sem):
            staged[a, to] = by_head(a, to)
            pltpu.make_async_remote_copy(
                src_ref=staged.at[a, to],
                dst_ref=landed.at[a, shard],
                send_sem=sem,
                recv_sem=recv_one.at[a],
                device_id=(to, column),
                device_id_type=MESH,
            ).start()

        def across(i, carry):
            step = jnp.where(i % 2 == 1, (i + 1) // 2, N // 2 - i // 2)
            send(2 * lax.rem(chip + step, N // 2) + side, send_one.at[side, a])
            return carry

        lax.fori_loop(1, N // 2, across, 0)

        @pl.when(core == side)
        def _():
            landed[a, shard] = by_head(a, shard)

        @pl.when(core != side)
        def _():
            send(2 * chip + side, send_sibling.at[a])

    def sent(a, side):
        some = staged.at[a, pl.ds(0, N // 2 - 1)]
        pltpu.make_async_remote_copy(
            src_ref=some,
            dst_ref=some,
            send_sem=send_one.at[side, a],
            recv_sem=recv_one.at[a],
            device_id=(shard, column),
            device_id_type=MESH,
        ).wait_send()

    def wait_all(buffer, send_sem, recv_sem):
        whole = pltpu.make_async_remote_copy(
            src_ref=buffer,
            dst_ref=buffer,
            send_sem=send_sem,
            recv_sem=recv_sem,
            device_id=(shard, column),
            device_id_type=MESH,
        )
        whole.wait_recv()
        whole.wait_send()

    def second(a):
        pltpu.make_async_remote_copy(
            src_ref=staged.at[a, 0],
            dst_ref=landed.at[a, pl.ds(0, N - 1)],
            send_sem=send_sibling.at[a],
            recv_sem=recv_one.at[a],
            device_id=(shard, column),
            device_id_type=MESH,
        ).wait_recv()

        def regroup(pair, carry):
            both = landed[a, :, pl.ds(pl.multiple_of(pair * 16, 16), 16), :].astype(jnp.float32)
            regrouped[a, 2 * pair] = both[:, :SPAN].reshape(2, CHUNK, DIM).astype(jnp.bfloat16)
            regrouped[a, 2 * pair + 1] = both[:, SPAN:].reshape(2, CHUNK, DIM).astype(jnp.bfloat16)
            return carry

        lax.fori_loop(0, N // 2, regroup, 0)

        def send(i, carry):
            to = partner(column, i)
            pltpu.make_async_remote_copy(
                src_ref=regrouped.at[a, to],
                dst_ref=arrived[a].at[column],
                send_sem=send_two.at[a],
                recv_sem=recv_two.at[a],
                device_id=(shard, to),
                device_id_type=MESH,
            ).start()
            return carry

        lax.fori_loop(1, N, send, 0)
        arrived[a][column] = regrouped[a, column]

    def order(a):
        wait_all(arrived[a].at[pl.ds(0, N - 1)], send_two.at[a], recv_two.at[a])

        def place(p, carry):
            second_half = p // N
            piece = p // 2 + folded * (p + second_half * (2 * N - 1 - 2 * p) - p // 2)
            half = p % 2 + folded * (second_half - p % 2)
            ordered[a, pl.ds(pl.multiple_of(p * CHUNK, CHUNK), CHUNK), :] = arrived[a][piece, half]
            return carry

        lax.fori_loop(0, 2 * N, place, 0)

    def give(a):
        def send(i, carry):
            to = partner(column, i)
            low = 2 * to - folded * to
            high = 2 * to + 1 + folded * (2 * N - 2 - 3 * to)
            leaving[a, to, :CHUNK] = results[a, low]
            leaving[a, to, CHUNK:] = results[a, high]
            return carry

        lax.fori_loop(0, N, send, 0)
        own_columns = pl.ds(pl.multiple_of(column * DIM, DIM), DIM)

        def start(i, carry):
            to = partner(column, i)
            pltpu.make_async_remote_copy(
                src_ref=leaving.at[a, to],
                dst_ref=outs[a].at[:, own_columns],
                send_sem=send_out.at[a],
                recv_sem=recv_out.at[a],
                device_id=(shard, to),
                device_id_type=MESH,
            ).start()
            return carry

        lax.fori_loop(1, N, start, 0)
        own = pltpu.make_async_copy(leaving.at[a, column], outs[a].at[:, own_columns], own_sem.at[a])
        own.start()
        return own

    for load in loads:
        load.wait()
    for i, (a, side) in enumerate(ORDER):
        if i >= WINDOW:
            sent(*ORDER[i - WINDOW])
        first(a, side)
        if i >= FORWARD:
            pl.when(core == 0)(functools.partial(second, i - FORWARD))
    for a in range(len(ORDER) - FORWARD, 3):
        pl.when(core == 0)(functools.partial(second, a))
    for a in range(3):
        pl.when(core == 1)(functools.partial(second, a))
    own_up.wait()
    order(3)
    order(0)
    order(1)

    keys, queries, values, given = (ordered.at[a] for a in range(4))
    blocks = LEN // BLOCK

    def chunks(b):
        return slice(b * (BLOCK // CHUNK), (b + 1) * (BLOCK // CHUNK))

    def keep(a, b, rows):
        results[a, chunks(b)] = rows.astype(jnp.bfloat16).reshape(BLOCK // CHUNK, CHUNK, DIM)

    def alive(start):
        return start + lax.broadcasted_iota(jnp.int32, (BLOCK, 1), 0) < length

    def incoming(b):
        return jnp.where(alive(b * BLOCK), given[b * BLOCK : (b + 1) * BLOCK].astype(jnp.float32), 0.0)

    def add(total, b, term):
        if b == blocks - 1:
            total[...] = term
        else:
            total[:, : (b + 1) * BLOCK] += term

    for b in reversed(range(blocks)):
        start, stop = b * BLOCK, (b + 1) * BLOCK
        scores = dot(queries[start:stop], keys[:stop], ROWS_BY_ROWS)
        row = lax.broadcasted_iota(jnp.int32, (BLOCK, BLOCK), 0)
        col = lax.broadcasted_iota(jnp.int32, (BLOCK, BLOCK), 1)
        last = jnp.where(col <= row, scores[:, start:], MASKED)
        scores = jnp.concatenate([scores[:, :start], last], axis=1) if b else last
        peak = jnp.max(scores, axis=1, keepdims=True)
        block_weights = jnp.exp2((scores - peak) * (SCALE * LOG2E))
        scale = 1.0 / jnp.sum(block_weights, axis=1, keepdims=True)
        inverse[start:stop] = scale
        rounded = block_weights.astype(jnp.bfloat16)
        weights[start:stop, :stop] = rounded
        scaled_incoming = (incoming(b) * scale).T.astype(jnp.bfloat16)
        add(value_sum, b, dot(scaled_incoming, rounded, ROWS_BY_COLUMNS))
        keep(3, b, value_sum[:, start:stop].T)
    own = [give(3)]

    order(2)
    for b in range(blocks):
        start, stop = b * BLOCK, (b + 1) * BLOCK
        blended = dot(weights[start:stop, :stop], values[:stop], ROWS_BY_COLUMNS) * inverse[start:stop]
        keep(0, b, jnp.where(alive(start), blended, 0.0))
    own.append(give(0))

    for b in reversed(range(blocks)):
        start, stop = b * BLOCK, (b + 1) * BLOCK
        block_incoming = incoming(b)
        attended_rows = results[0, chunks(b)].reshape(BLOCK, DIM).astype(jnp.float32)
        row_dots = jnp.sum(block_incoming * attended_rows, axis=1, keepdims=True)
        dweights = dot(block_incoming.astype(jnp.bfloat16), values[:stop], ROWS_BY_ROWS)
        dscores = (weights[start:stop, :stop].astype(jnp.float32) * (dweights - row_dots)).astype(jnp.bfloat16)
        weights[start:stop, :stop] = dscores
        keep(1, b, dot(dscores, keys[:stop], ROWS_BY_COLUMNS) * (inverse[start:stop] * SCALE))
    own.append(give(1))

    for b in reversed(range(blocks)):
        start, stop = b * BLOCK, (b + 1) * BLOCK
        scaled_queries = (queries[start:stop].astype(jnp.float32) * inverse[start:stop]).T.astype(jnp.bfloat16)
        add(key_sum, b, dot(scaled_queries, weights[start:stop, :stop], ROWS_BY_COLUMNS))
        keep(2, b, (key_sum[:, start:stop] * SCALE).T)
    own.append(give(2))

    for i in range(len(ORDER) - WINDOW, len(ORDER)):
        sent(*ORDER[i])
    for a in range(3):
        pltpu.make_async_remote_copy(
            src_ref=staged.at[a, 0],
            dst_ref=staged.at[a, 0],
            send_sem=send_sibling.at[a],
            recv_sem=recv_one.at[a],
            device_id=(shard, column),
            device_id_type=MESH,
        ).wait_send()
    for copy in own:
        copy.wait()
    for a in range(4):
        wait_all(outs[a].at[:, pl.ds(0, (N - 1) * DIM)], send_out.at[a], recv_out.at[a])


def per_device(queries_in, keys_in, values_in, upstream, lengths, assignment, span_order):
    flat = [x.reshape(N // 2, 2 * SPAN, FEAT) for x in (keys_in, queries_in, values_in)]
    smem = pl.BlockSpec(memory_space=pltpu.SMEM)
    anywhere = pl.BlockSpec(memory_space=pl.ANY)
    bf16, f32 = jnp.bfloat16, jnp.float32
    results = pl.pallas_call(
        kernel,
        out_shape=[pltpu.VMEM((ROWS, FEAT), bf16)] * 4,
        in_specs=[smem] * 3 + [anywhere] * 4,
        out_specs=[pl.BlockSpec(memory_space=pltpu.VMEM)] * 4,
        scratch_shapes=[
            pltpu.SMEM((N,), jnp.int32),
            pltpu.VMEM((N // 2, 2 * SPAN, FEAT), bf16),
            pltpu.VMEM((N // 2, 2 * SPAN, FEAT), bf16),
            pltpu.VMEM((N // 2, 2 * SPAN, FEAT), bf16),
            pltpu.VMEM((3, N, ROWS, DIM), bf16),
            pltpu.VMEM((3, N, ROWS, DIM), bf16),
            pltpu.VMEM((3, N, 2, CHUNK, DIM), bf16),
            pltpu.VMEM((N, 2, CHUNK, DIM), bf16),
            pltpu.VMEM((N, 2, CHUNK, DIM), bf16),
            pltpu.VMEM((N, 2, CHUNK, DIM), bf16),
            pltpu.VMEM((N, 2, CHUNK, DIM), bf16),
            pltpu.VMEM((4, LEN, DIM), bf16),
            pltpu.VMEM((LEN, LEN), bf16),
            pltpu.VMEM((LEN, 1), f32),
            pltpu.VMEM((DIM, LEN), f32),
            pltpu.VMEM((DIM, LEN), f32),
            pltpu.VMEM((4, LEN // CHUNK, CHUNK, DIM), bf16),
            pltpu.VMEM((4, N, ROWS, DIM), bf16),
            pltpu.SemaphoreType.DMA((3,)),
            pltpu.SemaphoreType.DMA,
            pltpu.SemaphoreType.DMA((2, 3)),
            pltpu.SemaphoreType.DMA((3,)),
            pltpu.SemaphoreType.DMA((3,)),
            pltpu.SemaphoreType.DMA((4,)),
            pltpu.SemaphoreType.DMA((4,)),
            pltpu.SemaphoreType.DMA((4,)),
            pltpu.SemaphoreType.DMA((4,)),
            pltpu.SemaphoreType.DMA((4,)),
        ],
        compiler_params=pltpu.CompilerParams(
            collective_id=0, has_side_effects=True, vmem_limit_bytes=52 * 1024 * 1024
        ),
    )(assignment, lengths, span_order, *flat, upstream.reshape(2, CHUNK, FEAT))
    return tuple(x.reshape(1, ROWS, FEAT) for x in results)


def solution(mesh):
    split = P("dp", None, "ctx", None)
    rows = P("dp", "ctx", None)
    return jax.shard_map(
        per_device,
        mesh=mesh,
        in_specs=(split, split, split, rows, P(), P(), P()),
        out_specs=(rows,) * 4,
        check_vma=False,
    )
```

```python
import math

import jax
import jax.numpy as jnp
from jax import lax
from jax.experimental import pallas as pl
from jax.experimental.pallas import tpu as pltpu
from jax.sharding import PartitionSpec as P

MESH = pl.DeviceIdType.MESH
N = 16
DIM = 128
ROWS = 128
LEN = 2048
FEAT = 2048
SPAN = 8
CHUNK = 64
BLOCK = 512
PLAN = (
    (1, 0, 0), (1, 1, 0), (2, 0, 0), (1, 2, 0), (2, 1, 0), (1, 0, 1), (2, 2, 0),
    (1, 1, 1), (1, 3, 0), (2, 0, 1), (1, 2, 1), (2, 1, 1), (2, 2, 1),
)
SCALE = 1.0 / math.sqrt(DIM)
LOG2E = math.log2(math.e)
MASKED = -1e30
ROWS_BY_ROWS = (((1,), (1,)), ((), ()))
ROWS_BY_COLUMNS = (((1,), (0,)), ((), ()))


def dot(left, right, dims):
    return lax.dot_general(left, right, dims, preferred_element_type=jnp.float32)


def partner(me, i):
    step = jnp.where(i % 2 == 1, (i + 1) // 2, N - i // 2)
    return lax.rem(me + step, N)


def kernel(
    assignment, lengths, span_order, keys_in, queries_in, values_in, upstream,
    attended, query_grad, key_grad, value_grad,
    sources, held_k, held_q, held_v, packed, landed, staged, arrived_k, arrived_q, arrived_v, arrived_g, pieces,
    ordered, weights, inverse,
    key_sum, value_sum, results, leaving,
    held_sem, up_sem, send_x, recv_x, send_z, send_sibling, recv_z, send_up, recv_up, send_out, recv_out, own_sem,
):
    shard = lax.axis_index("dp")
    column = lax.axis_index("ctx")
    ins = (keys_in, queries_in, values_in)
    outs = (attended, query_grad, key_grad, value_grad)
    held = (held_k, held_q, held_v)
    arrived = (arrived_k, arrived_q, arrived_v, arrived_g)

    loads = [pltpu.make_async_copy(ins[a], held[a], held_sem.at[a]) for a in range(3)]
    for load in loads:
        load.start()

    barrier = pltpu.get_barrier_semaphore()

    def greet(k, carry):
        pl.semaphore_signal(barrier, inc=1, device_id=(lax.rem(shard + k, N), column), device_id_type=MESH)
        pl.semaphore_signal(barrier, inc=1, device_id=(shard, lax.rem(column + k, N)), device_id_type=MESH)
        return carry

    lax.fori_loop(1, N, greet, 0)

    def find(d, carry):
        found = jnp.int32(0)
        for e in range(N):
            found = found + e * (assignment[e] == d).astype(jnp.int32)
        sources[d] = jnp.minimum(found, N - 1)
        return carry

    lax.fori_loop(0, N, find, 0)
    episode = sources[shard]
    length = lengths[episode]
    folded = jnp.clip(2 - lax.div(span_order[episode, 1], SPAN), 0, 1)
    pl.semaphore_wait(barrier, 2 * (N - 1))

    def send_upstream(i, carry):
        to = partner(column, i)
        pltpu.make_async_remote_copy(
            src_ref=upstream.at[:, :, pl.ds(pl.multiple_of(to * DIM, DIM), DIM)],
            dst_ref=arrived[3].at[column],
            send_sem=send_up,
            recv_sem=recv_up,
            device_id=(shard, to),
            device_id_type=MESH,
        ).start()
        return carry

    own_up = pltpu.make_async_copy(
        upstream.at[:, :, pl.ds(pl.multiple_of(column * DIM, DIM), DIM)], arrived[3].at[column], up_sem
    )
    own_up.start()

    core = lax.rem(shard, 2)
    chip = lax.div(shard, 2)

    def rows_of(a, to):
        e = sources[to]
        pair = held[a][lax.div(e, 2)].astype(jnp.float32)
        odd = jnp.full((SPAN, FEAT), lax.rem(e, 2), jnp.int32) == 1
        return jnp.where(odd, pair[SPAN:], pair[:SPAN])

    def first(a, side):
        for q in range(N // 4):
            both = jnp.concatenate([rows_of(a, 4 * q + side), rows_of(a, 4 * q + 2 + side)], axis=0).astype(jnp.bfloat16)
            for h in range(N):
                packed[a, side, h, 16 * q : 16 * q + 16] = both[:, h * DIM : (h + 1) * DIM]

        def send(i, carry):
            to = partner(column, i)
            pltpu.make_async_remote_copy(
                src_ref=packed.at[a, side, to],
                dst_ref=landed.at[a, side, column],
                send_sem=send_x.at[side, a],
                recv_sem=recv_x.at[side, a],
                device_id=(shard, to),
                device_id_type=MESH,
            ).start()
            return carry

        lax.fori_loop(1, N, send, 0)
        landed[a, side, column] = packed[a, side, column]

    def wait_all(buffer, send_sem, recv_sem):
        whole = pltpu.make_async_remote_copy(
            src_ref=buffer,
            dst_ref=buffer,
            send_sem=send_sem,
            recv_sem=recv_sem,
            device_id=(shard, column),
            device_id_type=MESH,
        )
        whole.wait_recv()
        whole.wait_send()

    def second(a, side):
        wait_all(landed.at[a, side, pl.ds(0, N - 1)], send_x.at[side, a], recv_x.at[side, a])
        for q in range(N // 4):
            both = landed[a, side, :, 16 * q : 16 * q + 16].astype(jnp.float32)
            staged[a, 4 * q + side] = both[:, :SPAN].reshape(ROWS, DIM).astype(jnp.bfloat16)
            staged[a, 4 * q + 2 + side] = both[:, SPAN:].reshape(ROWS, DIM).astype(jnp.bfloat16)

        def send(to, sem):
            pltpu.make_async_remote_copy(
                src_ref=staged.at[a, to],
                dst_ref=arrived[a].at[shard],
                send_sem=sem,
                recv_sem=recv_z.at[a],
                device_id=(to, column),
                device_id_type=MESH,
            ).start()

        def across(i, carry):
            step = jnp.where(i % 2 == 1, (i + 1) // 2, N // 2 - i // 2)
            send(2 * lax.rem(chip + step, N // 2) + side, send_z.at[side, a])
            return carry

        lax.fori_loop(1, N // 2, across, 0)

        @pl.when(core == side)
        def _():
            arrived[a][shard] = staged[a, shard]

        @pl.when(core != side)
        def _():
            send(2 * chip + side, send_sibling.at[a])

    def one_way(source, target, send_sem, recv_sem):
        return pltpu.make_async_remote_copy(
            src_ref=source,
            dst_ref=target,
            send_sem=send_sem,
            recv_sem=recv_sem,
            device_id=(shard, column),
            device_id_type=MESH,
        )

    def sent(a):
        some = staged.at[a, pl.ds(0, N // 2 - 1)]
        for side in range(2):
            one_way(some, some, send_z.at[side, a], recv_z.at[a]).wait_send()
        one_way(staged.at[a, 0], staged.at[a, 0], send_sibling.at[a], recv_z.at[a]).wait_send()

    def sort(a, source):
        for p in range(2 * N):
            second_half = p // N
            piece = p // 2 + folded * (p + second_half * (2 * N - 1 - 2 * p) - p // 2)
            half = p % 2 + folded * (second_half - p % 2)
            ordered[a, p * CHUNK : (p + 1) * CHUNK] = source[piece, half]

    def order(a):
        if a == 3:
            own_up.wait()
            wait_all(arrived[3].at[pl.ds(0, N - 1)], send_up, recv_up)
            sort(3, arrived[3])
            return
        some = arrived[a].at[pl.ds(0, N - 1)]
        one_way(some, some, send_z.at[0, a], recv_z.at[a]).wait_recv()
        for c in range(0, N, 2):
            both = arrived[a][:, c * SPAN : (c + 2) * SPAN].astype(jnp.float32)
            pieces[c] = both[:, :SPAN].reshape(2, CHUNK, DIM).astype(jnp.bfloat16)
            pieces[c + 1] = both[:, SPAN:].reshape(2, CHUNK, DIM).astype(jnp.bfloat16)
        sort(a, pieces)

    def give(a):
        for to in range(N):
            low = 2 * to - folded * to
            high = 2 * to + 1 + folded * (2 * N - 2 - 3 * to)
            leaving[a, to, :CHUNK] = results[a, low]
            leaving[a, to, CHUNK:] = results[a, high]
        own_columns = pl.ds(pl.multiple_of(column * DIM, DIM), DIM)

        def start(i, carry):
            to = partner(column, i)
            pltpu.make_async_remote_copy(
                src_ref=leaving.at[a, to],
                dst_ref=outs[a].at[:, own_columns],
                send_sem=send_out.at[a],
                recv_sem=recv_out.at[a],
                device_id=(shard, to),
                device_id_type=MESH,
            ).start()
            return carry

        lax.fori_loop(1, N, start, 0)
        own = pltpu.make_async_copy(leaving.at[a, column], outs[a].at[:, own_columns], own_sem.at[a])
        own.start()
        return own

    for load in loads:
        load.wait()
    for todo, a, side in PLAN:
        if todo == 2:
            second(a, side)
        elif a < 3:
            first(a, side)
        else:
            lax.fori_loop(1, N, send_upstream, 0)
    order(0)
    order(1)
    order(3)

    keys, queries, values, given = (ordered.at[a] for a in range(4))
    blocks = LEN // BLOCK

    def chunks(b):
        return slice(b * (BLOCK // CHUNK), (b + 1) * (BLOCK // CHUNK))

    def keep(a, b, rows):
        results[a, chunks(b)] = rows.astype(jnp.bfloat16).reshape(BLOCK // CHUNK, CHUNK, DIM)

    def alive(start):
        return start + lax.broadcasted_iota(jnp.int32, (BLOCK, 1), 0) < length

    def incoming(b):
        return jnp.where(alive(b * BLOCK), given[b * BLOCK : (b + 1) * BLOCK].astype(jnp.float32), 0.0)

    def add(total, b, term):
        if b == blocks - 1:
            total[...] = term
        else:
            total[:, : (b + 1) * BLOCK] += term

    for b in reversed(range(blocks)):
        start, stop = b * BLOCK, (b + 1) * BLOCK
        scores = dot(queries[start:stop], keys[:stop], ROWS_BY_ROWS)
        row = lax.broadcasted_iota(jnp.int32, (BLOCK, BLOCK), 0)
        col = lax.broadcasted_iota(jnp.int32, (BLOCK, BLOCK), 1)
        last = jnp.where(col <= row, scores[:, start:], MASKED)
        scores = jnp.concatenate([scores[:, :start], last], axis=1) if b else last
        peak = jnp.max(scores, axis=1, keepdims=True)
        block_weights = jnp.exp2((scores - peak) * (SCALE * LOG2E))
        inverse[start:stop] = 1.0 / jnp.sum(block_weights, axis=1, keepdims=True)
        rounded = block_weights.astype(jnp.bfloat16)
        weights[start:stop, :stop] = rounded

    for b in reversed(range(blocks)):
        start, stop = b * BLOCK, (b + 1) * BLOCK
        scaled_incoming = (incoming(b) * inverse[start:stop]).T.astype(jnp.bfloat16)
        add(value_sum, b, dot(scaled_incoming, weights[start:stop, :stop], ROWS_BY_COLUMNS))
        keep(3, b, value_sum[:, start:stop].T)
    own = [give(3)]

    order(2)
    for b in range(blocks):
        start, stop = b * BLOCK, (b + 1) * BLOCK
        blended = dot(weights[start:stop, :stop], values[:stop], ROWS_BY_COLUMNS) * inverse[start:stop]
        keep(0, b, jnp.where(alive(start), blended, 0.0))
    own.append(give(0))

    for b in reversed(range(blocks)):
        start, stop = b * BLOCK, (b + 1) * BLOCK
        block_incoming = incoming(b)
        attended_rows = results[0, chunks(b)].reshape(BLOCK, DIM).astype(jnp.float32)
        row_dots = jnp.sum(block_incoming * attended_rows, axis=1, keepdims=True)
        dweights = dot(block_incoming.astype(jnp.bfloat16), values[:stop], ROWS_BY_ROWS)
        dscores = (weights[start:stop, :stop].astype(jnp.float32) * (dweights - row_dots)).astype(jnp.bfloat16)
        weights[start:stop, :stop] = dscores
        keep(1, b, dot(dscores, keys[:stop], ROWS_BY_COLUMNS) * (inverse[start:stop] * SCALE))
    own.append(give(1))

    for b in reversed(range(blocks)):
        start, stop = b * BLOCK, (b + 1) * BLOCK
        scaled_queries = (queries[start:stop].astype(jnp.float32) * inverse[start:stop]).T.astype(jnp.bfloat16)
        add(key_sum, b, dot(scaled_queries, weights[start:stop, :stop], ROWS_BY_COLUMNS))
        keep(2, b, (key_sum[:, start:stop] * SCALE).T)
    own.append(give(2))

    for a in range(3):
        sent(a)
    for copy in own:
        copy.wait()
    for a in range(4):
        wait_all(outs[a].at[:, pl.ds(0, (N - 1) * DIM)], send_out.at[a], recv_out.at[a])


def per_device(queries_in, keys_in, values_in, upstream, lengths, assignment, span_order):
    flat = [x.reshape(N // 2, 2 * SPAN, FEAT) for x in (keys_in, queries_in, values_in)]
    smem = pl.BlockSpec(memory_space=pltpu.SMEM)
    anywhere = pl.BlockSpec(memory_space=pl.ANY)
    bf16, f32 = jnp.bfloat16, jnp.float32
    results = pl.pallas_call(
        kernel,
        out_shape=[pltpu.VMEM((ROWS, FEAT), bf16)] * 4,
        in_specs=[smem] * 3 + [anywhere] * 4,
        out_specs=[pl.BlockSpec(memory_space=pltpu.VMEM)] * 4,
        scratch_shapes=[
            pltpu.SMEM((N,), jnp.int32),
            pltpu.VMEM((N // 2, 2 * SPAN, FEAT), bf16),
            pltpu.VMEM((N // 2, 2 * SPAN, FEAT), bf16),
            pltpu.VMEM((N // 2, 2 * SPAN, FEAT), bf16),
            pltpu.VMEM((3, 2, N, CHUNK, DIM), bf16),
            pltpu.VMEM((3, 2, N, CHUNK, DIM), bf16),
            pltpu.VMEM((3, N, ROWS, DIM), bf16),
            pltpu.VMEM((N, ROWS, DIM), bf16),
            pltpu.VMEM((N, ROWS, DIM), bf16),
            pltpu.VMEM((N, ROWS, DIM), bf16),
            pltpu.VMEM((N, 2, CHUNK, DIM), bf16),
            pltpu.VMEM((N, 2, CHUNK, DIM), bf16),
            pltpu.VMEM((4, LEN, DIM), bf16),
            pltpu.VMEM((LEN, LEN), bf16),
            pltpu.VMEM((LEN, 1), f32),
            pltpu.VMEM((DIM, LEN), f32),
            pltpu.VMEM((DIM, LEN), f32),
            pltpu.VMEM((4, LEN // CHUNK, CHUNK, DIM), bf16),
            pltpu.VMEM((4, N, ROWS, DIM), bf16),
            pltpu.SemaphoreType.DMA((3,)),
            pltpu.SemaphoreType.DMA,
            pltpu.SemaphoreType.DMA((2, 3)),
            pltpu.SemaphoreType.DMA((2, 3)),
            pltpu.SemaphoreType.DMA((2, 3)),
            pltpu.SemaphoreType.DMA((3,)),
            pltpu.SemaphoreType.DMA((3,)),
            pltpu.SemaphoreType.DMA,
            pltpu.SemaphoreType.DMA,
            pltpu.SemaphoreType.DMA((4,)),
            pltpu.SemaphoreType.DMA((4,)),
            pltpu.SemaphoreType.DMA((4,)),
        ],
        compiler_params=pltpu.CompilerParams(
            collective_id=0, has_side_effects=True, vmem_limit_bytes=52 * 1024 * 1024
        ),
    )(assignment, lengths, span_order, *flat, upstream.reshape(2, CHUNK, FEAT))
    return tuple(x.reshape(1, ROWS, FEAT) for x in results)


def solution(mesh):
    split = P("dp", None, "ctx", None)
    rows = P("dp", "ctx", None)
    return jax.shard_map(
        per_device,
        mesh=mesh,
        in_specs=(split, split, split, rows, P(), P(), P()),
        out_specs=(rows,) * 4,
        check_vma=False,
    )
```

```python
import math

import jax
import jax.numpy as jnp
from jax import lax
from jax.experimental import pallas as pl
from jax.experimental.pallas import tpu as pltpu
from jax.sharding import PartitionSpec as P

MESH = pl.DeviceIdType.MESH
N = 16
DIM = 128
ROWS = 128
LEN = 2048
FEAT = 2048
SPAN = 8
CHUNK = 64
SCORE_BLOCK = 256
QUERY_BLOCK = 512
VALUE_BLOCK = 512
PLAN = (
    (1, 0, 0), (1, 1, 0), (2, 0, 0), (1, 2, 0), (2, 1, 0), (1, 0, 1), (2, 2, 0),
    (1, 1, 1), (1, 3, 0), (2, 0, 1), (1, 2, 1), (2, 1, 1), (2, 2, 1),
)
SCALE = 1.0 / math.sqrt(DIM)
LOG2E = math.log2(math.e)
MASKED = -1e30
ROWS_BY_ROWS = (((1,), (1,)), ((), ()))
ROWS_BY_COLUMNS = (((1,), (0,)), ((), ()))


def dot(left, right, dims):
    return lax.dot_general(left, right, dims, preferred_element_type=jnp.float32)


def partner(me, i):
    step = jnp.where(i % 2 == 1, (i + 1) // 2, N - i // 2)
    return lax.rem(me + step, N)


def kernel(
    assignment, lengths, span_order, keys_in, queries_in, values_in, upstream,
    attended, query_grad, key_grad, value_grad,
    sources, held_k, held_q, held_v, packed, landed, staged, arrived_k, arrived_q, arrived_v, arrived_g, pieces,
    ordered, weights, inverse,
    key_sum, value_sum, results, leaving,
    held_sem, up_sem, send_x, recv_x, send_z, send_sibling, recv_z, send_up, recv_up, send_out, recv_out, own_sem,
):
    shard = lax.axis_index("dp")
    column = lax.axis_index("ctx")
    ins = (keys_in, queries_in, values_in)
    outs = (attended, query_grad, key_grad, value_grad)
    held = (held_k, held_q, held_v)
    arrived = (arrived_k, arrived_q, arrived_v, arrived_g)

    loads = [pltpu.make_async_copy(ins[a], held[a], held_sem.at[a]) for a in range(3)]
    for load in loads:
        load.start()

    barrier = pltpu.get_barrier_semaphore()

    def greet(k, carry):
        pl.semaphore_signal(barrier, inc=1, device_id=(lax.rem(shard + k, N), column), device_id_type=MESH)
        pl.semaphore_signal(barrier, inc=1, device_id=(shard, lax.rem(column + k, N)), device_id_type=MESH)
        return carry

    lax.fori_loop(1, N, greet, 0)

    def find(d, carry):
        found = jnp.int32(0)
        for e in range(N):
            found = found + e * (assignment[e] == d).astype(jnp.int32)
        sources[d] = jnp.minimum(found, N - 1)
        return carry

    lax.fori_loop(0, N, find, 0)
    episode = sources[shard]
    length = lengths[episode]
    folded = jnp.clip(2 - lax.div(span_order[episode, 1], SPAN), 0, 1)
    pl.semaphore_wait(barrier, 2 * (N - 1))

    def send_upstream(i, carry):
        to = partner(column, i)
        pltpu.make_async_remote_copy(
            src_ref=upstream.at[:, :, pl.ds(pl.multiple_of(to * DIM, DIM), DIM)],
            dst_ref=arrived[3].at[column],
            send_sem=send_up,
            recv_sem=recv_up,
            device_id=(shard, to),
            device_id_type=MESH,
        ).start()
        return carry

    own_up = pltpu.make_async_copy(
        upstream.at[:, :, pl.ds(pl.multiple_of(column * DIM, DIM), DIM)], arrived[3].at[column], up_sem
    )
    own_up.start()

    core = lax.rem(shard, 2)
    chip = lax.div(shard, 2)

    def rows_of(a, to):
        e = sources[to]
        pair = held[a][lax.div(e, 2)].astype(jnp.float32)
        odd = jnp.full((SPAN, FEAT), lax.rem(e, 2), jnp.int32) == 1
        return jnp.where(odd, pair[SPAN:], pair[:SPAN])

    def first(a, side):
        for q in range(N // 4):
            both = jnp.concatenate([rows_of(a, 4 * q + side), rows_of(a, 4 * q + 2 + side)], axis=0).astype(jnp.bfloat16)
            for h in range(N):
                packed[a, side, h, 16 * q : 16 * q + 16] = both[:, h * DIM : (h + 1) * DIM]

        def send(i, carry):
            to = partner(column, i)
            pltpu.make_async_remote_copy(
                src_ref=packed.at[a, side, to],
                dst_ref=landed.at[a, side, column],
                send_sem=send_x.at[side, a],
                recv_sem=recv_x.at[side, a],
                device_id=(shard, to),
                device_id_type=MESH,
            ).start()
            return carry

        lax.fori_loop(1, N, send, 0)
        landed[a, side, column] = packed[a, side, column]

    def wait_all(buffer, send_sem, recv_sem):
        whole = pltpu.make_async_remote_copy(
            src_ref=buffer,
            dst_ref=buffer,
            send_sem=send_sem,
            recv_sem=recv_sem,
            device_id=(shard, column),
            device_id_type=MESH,
        )
        whole.wait_recv()
        whole.wait_send()

    def second(a, side):
        wait_all(landed.at[a, side, pl.ds(0, N - 1)], send_x.at[side, a], recv_x.at[side, a])
        for q in range(N // 4):
            both = landed[a, side, :, 16 * q : 16 * q + 16].astype(jnp.float32)
            staged[a, 4 * q + side] = both[:, :SPAN].reshape(ROWS, DIM).astype(jnp.bfloat16)
            staged[a, 4 * q + 2 + side] = both[:, SPAN:].reshape(ROWS, DIM).astype(jnp.bfloat16)

        def send(to, sem):
            pltpu.make_async_remote_copy(
                src_ref=staged.at[a, to],
                dst_ref=arrived[a].at[shard],
                send_sem=sem,
                recv_sem=recv_z.at[a],
                device_id=(to, column),
                device_id_type=MESH,
            ).start()

        def across(i, carry):
            step = jnp.where(i % 2 == 1, (i + 1) // 2, N // 2 - i // 2)
            send(2 * lax.rem(chip + step, N // 2) + side, send_z.at[side, a])
            return carry

        lax.fori_loop(1, N // 2, across, 0)

        @pl.when(core == side)
        def _():
            arrived[a][shard] = staged[a, shard]

        @pl.when(core != side)
        def _():
            send(2 * chip + side, send_sibling.at[a])

    def one_way(source, target, send_sem, recv_sem):
        return pltpu.make_async_remote_copy(
            src_ref=source,
            dst_ref=target,
            send_sem=send_sem,
            recv_sem=recv_sem,
            device_id=(shard, column),
            device_id_type=MESH,
        )

    def sent(a):
        some = staged.at[a, pl.ds(0, N // 2 - 1)]
        for side in range(2):
            one_way(some, some, send_z.at[side, a], recv_z.at[a]).wait_send()
        one_way(staged.at[a, 0], staged.at[a, 0], send_sibling.at[a], recv_z.at[a]).wait_send()

    def sort(a, source):
        for p in range(2 * N):
            second_half = p // N
            piece = p // 2 + folded * (p + second_half * (2 * N - 1 - 2 * p) - p // 2)
            half = p % 2 + folded * (second_half - p % 2)
            ordered[a, p * CHUNK : (p + 1) * CHUNK] = source[piece, half]

    def order(a):
        if a == 3:
            own_up.wait()
            wait_all(arrived[3].at[pl.ds(0, N - 1)], send_up, recv_up)
            sort(3, arrived[3])
            return
        some = arrived[a].at[pl.ds(0, N - 1)]
        one_way(some, some, send_z.at[0, a], recv_z.at[a]).wait_recv()
        for c in range(0, N, 2):
            both = arrived[a][:, c * SPAN : (c + 2) * SPAN].astype(jnp.float32)
            pieces[c] = both[:, :SPAN].reshape(2, CHUNK, DIM).astype(jnp.bfloat16)
            pieces[c + 1] = both[:, SPAN:].reshape(2, CHUNK, DIM).astype(jnp.bfloat16)
        sort(a, pieces)

    def give(a):
        for to in range(N):
            low = 2 * to - folded * to
            high = 2 * to + 1 + folded * (2 * N - 2 - 3 * to)
            leaving[a, to, :CHUNK] = results[a, low]
            leaving[a, to, CHUNK:] = results[a, high]
        own_columns = pl.ds(pl.multiple_of(column * DIM, DIM), DIM)

        def start(i, carry):
            to = partner(column, i)
            pltpu.make_async_remote_copy(
                src_ref=leaving.at[a, to],
                dst_ref=outs[a].at[:, own_columns],
                send_sem=send_out.at[a],
                recv_sem=recv_out.at[a],
                device_id=(shard, to),
                device_id_type=MESH,
            ).start()
            return carry

        lax.fori_loop(1, N, start, 0)
        own = pltpu.make_async_copy(leaving.at[a, column], outs[a].at[:, own_columns], own_sem.at[a])
        own.start()
        return own

    for load in loads:
        load.wait()
    for todo, a, side in PLAN:
        if todo == 2:
            second(a, side)
        elif a < 3:
            first(a, side)
        else:
            lax.fori_loop(1, N, send_upstream, 0)
    order(0)
    order(1)
    order(3)

    keys, queries, values, given = (ordered.at[a] for a in range(4))

    def spans(size):
        return [(start, start + size) for start in reversed(range(0, LEN, size))]

    def keep(a, start, rows):
        some = rows.shape[0] // CHUNK
        results[a, start // CHUNK : start // CHUNK + some] = rows.astype(jnp.bfloat16).reshape(some, CHUNK, DIM)

    def alive(start, stop):
        return start + lax.broadcasted_iota(jnp.int32, (stop - start, 1), 0) < length

    def incoming(start, stop):
        return jnp.where(alive(start, stop), given[start:stop].astype(jnp.float32), 0.0)

    def add(total, stop, term):
        if stop == LEN:
            total[...] = term
        else:
            total[:, :stop] += term

    for start, stop in spans(SCORE_BLOCK):
        scores = dot(queries[start:stop], keys[:stop], ROWS_BY_ROWS)
        row = lax.broadcasted_iota(jnp.int32, (SCORE_BLOCK, SCORE_BLOCK), 0)
        col = lax.broadcasted_iota(jnp.int32, (SCORE_BLOCK, SCORE_BLOCK), 1)
        last = jnp.where(col <= row, scores[:, start:], MASKED)
        scores = jnp.concatenate([scores[:, :start], last], axis=1) if start else last
        peak = jnp.max(scores, axis=1, keepdims=True)
        block_weights = jnp.exp2((scores - peak) * (SCALE * LOG2E))
        inverse[start:stop] = 1.0 / jnp.sum(block_weights, axis=1, keepdims=True)
        weights[start:stop, :stop] = block_weights.astype(jnp.bfloat16)
        if SCORE_BLOCK < VALUE_BLOCK and start % VALUE_BLOCK + SCORE_BLOCK < VALUE_BLOCK:
            weights[start:stop, stop : start - start % VALUE_BLOCK + VALUE_BLOCK] = jnp.zeros(
                (SCORE_BLOCK, VALUE_BLOCK - start % VALUE_BLOCK - SCORE_BLOCK), jnp.bfloat16
            )

    for start, stop in spans(VALUE_BLOCK):
        scaled_incoming = (incoming(start, stop) * inverse[start:stop]).T.astype(jnp.bfloat16)
        add(value_sum, stop, dot(scaled_incoming, weights[start:stop, :stop], ROWS_BY_COLUMNS))
        keep(3, start, value_sum[:, start:stop].T)
    own = [give(3)]

    order(2)
    for start, stop in spans(VALUE_BLOCK):
        blended = dot(weights[start:stop, :stop], values[:stop], ROWS_BY_COLUMNS) * inverse[start:stop]
        keep(0, start, jnp.where(alive(start, stop), blended, 0.0))
    own.append(give(0))

    for start, stop in spans(QUERY_BLOCK):
        block_incoming = incoming(start, stop)
        attended_rows = results[0, start // CHUNK : stop // CHUNK].reshape(QUERY_BLOCK, DIM).astype(jnp.float32)
        row_dots = jnp.sum(block_incoming * attended_rows, axis=1, keepdims=True)
        dweights = dot(block_incoming.astype(jnp.bfloat16), values[:stop], ROWS_BY_ROWS)
        dscores = (weights[start:stop, :stop].astype(jnp.float32) * (dweights - row_dots)).astype(jnp.bfloat16)
        weights[start:stop, :stop] = dscores
        keep(1, start, dot(dscores, keys[:stop], ROWS_BY_COLUMNS) * (inverse[start:stop] * SCALE))
    own.append(give(1))

    for start, stop in spans(VALUE_BLOCK):
        scaled_queries = (queries[start:stop].astype(jnp.float32) * inverse[start:stop]).T.astype(jnp.bfloat16)
        add(key_sum, stop, dot(scaled_queries, weights[start:stop, :stop], ROWS_BY_COLUMNS))
        keep(2, start, (key_sum[:, start:stop] * SCALE).T)
    own.append(give(2))

    for a in range(3):
        sent(a)
    for copy in own:
        copy.wait()
    for a in range(4):
        wait_all(outs[a].at[:, pl.ds(0, (N - 1) * DIM)], send_out.at[a], recv_out.at[a])


def per_device(queries_in, keys_in, values_in, upstream, lengths, assignment, span_order):
    flat = [x.reshape(N // 2, 2 * SPAN, FEAT) for x in (keys_in, queries_in, values_in)]
    smem = pl.BlockSpec(memory_space=pltpu.SMEM)
    anywhere = pl.BlockSpec(memory_space=pl.ANY)
    bf16, f32 = jnp.bfloat16, jnp.float32
    results = pl.pallas_call(
        kernel,
        out_shape=[pltpu.VMEM((ROWS, FEAT), bf16)] * 4,
        in_specs=[smem] * 3 + [anywhere] * 4,
        out_specs=[pl.BlockSpec(memory_space=pltpu.VMEM)] * 4,
        scratch_shapes=[
            pltpu.SMEM((N,), jnp.int32),
            pltpu.VMEM((N // 2, 2 * SPAN, FEAT), bf16),
            pltpu.VMEM((N // 2, 2 * SPAN, FEAT), bf16),
            pltpu.VMEM((N // 2, 2 * SPAN, FEAT), bf16),
            pltpu.VMEM((3, 2, N, CHUNK, DIM), bf16),
            pltpu.VMEM((3, 2, N, CHUNK, DIM), bf16),
            pltpu.VMEM((3, N, ROWS, DIM), bf16),
            pltpu.VMEM((N, ROWS, DIM), bf16),
            pltpu.VMEM((N, ROWS, DIM), bf16),
            pltpu.VMEM((N, ROWS, DIM), bf16),
            pltpu.VMEM((N, 2, CHUNK, DIM), bf16),
            pltpu.VMEM((N, 2, CHUNK, DIM), bf16),
            pltpu.VMEM((4, LEN, DIM), bf16),
            pltpu.VMEM((LEN, LEN), bf16),
            pltpu.VMEM((LEN, 1), f32),
            pltpu.VMEM((DIM, LEN), f32),
            pltpu.VMEM((DIM, LEN), f32),
            pltpu.VMEM((4, LEN // CHUNK, CHUNK, DIM), bf16),
            pltpu.VMEM((4, N, ROWS, DIM), bf16),
            pltpu.SemaphoreType.DMA((3,)),
            pltpu.SemaphoreType.DMA,
            pltpu.SemaphoreType.DMA((2, 3)),
            pltpu.SemaphoreType.DMA((2, 3)),
            pltpu.SemaphoreType.DMA((2, 3)),
            pltpu.SemaphoreType.DMA((3,)),
            pltpu.SemaphoreType.DMA((3,)),
            pltpu.SemaphoreType.DMA,
            pltpu.SemaphoreType.DMA,
            pltpu.SemaphoreType.DMA((4,)),
            pltpu.SemaphoreType.DMA((4,)),
            pltpu.SemaphoreType.DMA((4,)),
        ],
        compiler_params=pltpu.CompilerParams(
            collective_id=0, has_side_effects=True, vmem_limit_bytes=52 * 1024 * 1024
        ),
    )(assignment, lengths, span_order, *flat, upstream.reshape(2, CHUNK, FEAT))
    return tuple(x.reshape(1, ROWS, FEAT) for x in results)


def solution(mesh):
    split = P("dp", None, "ctx", None)
    rows = P("dp", "ctx", None)
    return jax.shard_map(
        per_device,
        mesh=mesh,
        in_specs=(split, split, split, rows, P(), P(), P()),
        out_specs=(rows,) * 4,
        check_vma=False,
    )
```
